32 devices in a mesh: groups: 2 (over y), hid: 4 (over z), wid: 4 (over x, core).
Axes of the slice: x: 2, y: 2, z: 4, core: 2. Of those that a mesh axis runs over, the one named last changes fastest.
Arguments:
- activations: bfloat16 [512, 8192], P(('groups', 'hid'), 'wid'), parts along dimension 0, may hold values from -50 to 50, as said below
- norm_gain: float32 [8192], P('wid'), may hold values from 0.1 to 1.9
- gate_weight: bfloat16 [8192, 28672], P('wid', 'hid'), may hold values from -0.0625 to 0.0625
- up_weight: bfloat16 [8192, 28672], P('wid', 'hid'), may hold values from -0.0625 to 0.0625
- down_weight: bfloat16 [28672, 8192], P('hid', 'wid'), may hold values from -0.0625 to 0.0625
Outputs:
- final_rows: bfloat16 [512, 8192], P(('groups', 'hid'), 'wid'), parts along dimension 0
The draws below stay inside these ranges and needn't reach their ends.
There are 2 independent parts, one for each index of `groups`. The reference program is written for one: setup_inputs(seed, part) draws one part's arguments, and reference() takes and returns one part's arrays. A program takes and returns all parts, laid end to end along the dimension named above; an argument that names none is the same for every part. Nothing has to cross between parts.
Inputs may be any that keep to these rules, and one draw needn't show every extreme that they name: real-valued activations.
All inputs are finite; a program needn't handle non-finite values.
Results may differ from the reference program's by a relative error of at most 0.019.
Values may be sent and summed in bfloat16 or wider, within the bound.
A program may use at most 192 MiB of HBM per device.

```python
import jax
import jax.numpy as jnp
from jax import lax

D = 8192
FF = 28672
ROWS = 256
N_WID = 4


def draw_activations(key, part):
    key = jax.random.fold_in(key, 11)
    key_base, key_rowsc, key_colsc = jax.random.split(key, 3)
    column_pos = jnp.arange(D, dtype=jnp.float32) / D
    base = jnp.clip(jax.random.normal(key_base, (ROWS, D), jnp.float32), -3.5, 3.5)
    row_log = jax.random.uniform(key_rowsc, (ROWS, 1), jnp.float32, 0.0, 1.0)
    col_log = 0.5 * column_pos[None, :] + 0.5 * jax.random.uniform(key_colsc, (1, D), jnp.float32, 0.0, 1.0)
    scales = jnp.power(10.0, row_log - 0.6) * jnp.power(10.0, col_log - 0.5)
    return (base * scales).astype(jnp.bfloat16)


def shard_levels(stream_key, extent, cuts, smallest, top_value):
    def one(axis_at, blocks):
        heights = jax.random.uniform(jax.random.fold_in(jax.random.fold_in(stream_key, 6), axis_at), (blocks,), jnp.float32, smallest / len(cuts), top_value / len(cuts))
        return jnp.repeat(jnp.exp(heights), extent[axis_at] // blocks).reshape((-1,) + (1,) * (len(extent) - axis_at - 1))

    gain = one(*cuts[0])
    for cut in cuts[1:]:
        gain = gain * one(*cut)
    return gain


def bell_draw(stream_key, extent, spread, bound, pieces=(), kind=jnp.bfloat16):
    values = spread * jax.random.normal(stream_key, extent, jnp.float32)
    if pieces:
        values = values * shard_levels(stream_key, extent, pieces, -0.22, 0.18)
    return jnp.clip(values, -bound, bound).astype(kind)


def setup_inputs(seed: int = 0, part: int = 0) -> dict:
    seeds = jax.random.split(jax.random.key(seed), 6)
    part_splits = jax.random.split(jax.random.fold_in(seeds[5], part), 6)
    return {
        "activations": draw_activations(jax.random.fold_in(jax.random.fold_in(seeds[5], part), 71), part),
        "norm_gain": jnp.clip(1.0 + 0.18 * jax.random.normal(seeds[1], (D,), jnp.float32), 0.1, 1.9),
        "gate_weight": bell_draw(seeds[2], (D, FF), D ** -0.5, 0.0625, ((0, 4), (1, 4))),
        "up_weight": bell_draw(seeds[3], (D, FF), D ** -0.5, 0.0625, ((0, 4), (1, 4))),
        "down_weight": bell_draw(seeds[4], (FF, D), (FF // 4) ** -0.5, 0.0625, ((0, 4), (1, 4))),
    }


def normed(values, norm_gain):
    wide = values.astype(jnp.float32)
    meansq = lax.optimization_barrier(jnp.mean(wide * wide, axis=1, keepdims=True))
    return (wide * jax.lax.rsqrt(meansq + 1e-05) * norm_gain[None, :]).astype(jnp.bfloat16)

def hidden_of(inputs, gate_weight, up_weight):
    width_block = D // N_WID
    gate_total = jnp.zeros((inputs.shape[0], FF), jnp.float32)
    up_total = jnp.zeros((inputs.shape[0], FF), jnp.float32)
    for block in range(N_WID):
        lower = block * width_block
        piece = inputs[:, lower:lower + width_block]
        gate_part = jnp.dot(piece, gate_weight[lower:lower + width_block], preferred_element_type=jnp.float32)
        up_part = jnp.dot(piece, up_weight[lower:lower + width_block], preferred_element_type=jnp.float32)
        gate_total = gate_total + gate_part.astype(jnp.bfloat16).astype(jnp.float32)
        up_total = up_total + up_part.astype(jnp.bfloat16).astype(jnp.float32)
    return (jax.nn.silu(gate_total) * up_total).astype(jnp.bfloat16)

def one_step(values, norm_gain, gate_weight, up_weight, down_weight):
    hidden = hidden_of(normed(values, norm_gain), gate_weight, up_weight)
    branch = jnp.dot(hidden, down_weight, preferred_element_type=jnp.float32)
    return (values.astype(jnp.float32) + branch).astype(jnp.bfloat16)

def reference(activations, norm_gain, gate_weight, up_weight, down_weight):
    first_rows = one_step(activations, norm_gain, gate_weight, up_weight, down_weight)
    return one_step(first_rows, norm_gain, gate_weight, up_weight, down_weight)
```

```python
import functools

import jax
import jax.numpy as jnp
from jax import lax
from jax.experimental import pallas as pl
from jax.experimental.pallas import tpu as pltpu
from jax.sharding import PartitionSpec as P

D = 8192
EPS = 1e-05
UNITS = 512
LAG2, LAG3, LAG4, LAG5 = 1, 3, 5, 6
LAG_ROWS, LAG_NORM = 4, 2
RING = 8


def normed(values, norm_gain):
    wide = values.astype(jnp.float32)
    partial_sq = jnp.sum(wide * wide, axis=1)
    total_sq = lax.psum(partial_sq, "wid")
    factor = lax.rsqrt(total_sq / D + EPS)
    return (wide * factor[:, None] * norm_gain[None, :]).astype(jnp.bfloat16)


def project_local(inputs, gate_weight, up_weight):
    gate_part = jnp.dot(inputs, gate_weight, preferred_element_type=jnp.float32)
    up_part = jnp.dot(inputs, up_weight, preferred_element_type=jnp.float32)
    return jnp.stack([gate_part, up_part]).astype(jnp.bfloat16).astype(jnp.float32)


def combine_hidden(partials):
    shared = lax.psum_scatter(
        partials.astype(jnp.bfloat16), "wid", scatter_dimension=2, tiled=True
    ).astype(jnp.float32)
    hidden_share = (jax.nn.silu(shared[0]) * shared[1]).astype(jnp.bfloat16)
    return lax.all_gather(hidden_share, "wid", axis=1, tiled=True)


def hidden_from_share(normed_share, gate_weight, up_weight):
    partials = project_local(
        lax.all_gather(normed_share, "hid", axis=0, tiled=True), gate_weight, up_weight
    )
    return combine_hidden(partials)


def down_share(hidden, down_weight):
    return lax.psum_scatter(
        jnp.dot(hidden, down_weight, preferred_element_type=jnp.float32).astype(jnp.bfloat16),
        "hid",
        scatter_dimension=0,
        tiled=True,
    ).astype(jnp.float32)


def plain_body(activations, norm_gain, gate_weight, up_weight, down_weight):
    first_hidden = hidden_from_share(normed(activations, norm_gain), gate_weight, up_weight)
    first_own = (activations.astype(jnp.float32) + down_share(first_hidden, down_weight)).astype(
        jnp.bfloat16
    )
    second_hidden = hidden_from_share(normed(first_own, norm_gain), gate_weight, up_weight)
    second_branch = down_share(second_hidden, down_weight)
    return (first_own.astype(jnp.float32) + second_branch).astype(jnp.bfloat16)


def kernel(
    chunks, x_ref, gain_ref, wg_hbm, wu_hbm, wd_hbm, out_ref,
    wgu, wd, rows, acts, part, recv_a, send_b, recv_b, hidden, acc, rs_send, rs_recv,
    stat_send, stat_recv,
    w_sem, wd_sem, sa_sem, ra_sem, sb_sem, rb_sem, sh_sem, rh_sem, sg_sem, rg_sem,
    srs_sem, rrs_sem, sag_sem, rag_sem, sst_sem, rst_sem,
):
    total = 4 * chunks
    h = lax.axis_index("hid")
    w = lax.axis_index("wid")
    chip, core = lax.div(w, 2), lax.rem(w, 2)
    other_core = 2 * chip + (1 - core)
    other_chip = 2 * (1 - chip) + core
    half_rows = rows.shape[1]
    width = rows.shape[2]

    def remote(src, dst, send, recv, axis, peer):
        return pltpu.make_async_remote_copy(
            src_ref=src, dst_ref=dst, send_sem=send, recv_sem=recv,
            device_id={axis: peer}, device_id_type=pl.DeviceIdType.MESH,
        )

    barrier = pltpu.get_barrier_semaphore()
    for d in (1, 2, 3):
        pl.semaphore_signal(barrier, inc=1, device_id={"wid": lax.rem(w + d, 4)},
                            device_id_type=pl.DeviceIdType.MESH)
        pl.semaphore_signal(barrier, inc=1, device_id={"hid": lax.rem(h + d, 4)},
                            device_id_type=pl.DeviceIdType.MESH)

    def weight_copies(g):
        columns = pl.ds(pl.multiple_of(lax.rem(g, chunks) * UNITS, UNITS), UNITS)
        slot = lax.rem(g, 2)
        return (
            pltpu.make_async_copy(wg_hbm.at[:, columns], wgu.at[slot, 0], w_sem.at[slot, 0]),
            pltpu.make_async_copy(wu_hbm.at[:, columns], wgu.at[slot, 1], w_sem.at[slot, 1]),
        )

    def down_copy(c):
        span = pl.ds(pl.multiple_of(c * UNITS, UNITS), UNITS)
        return pltpu.make_async_copy(wd_hbm.at[span, :], wd.at[c], wd_sem.at[c])

    def stat_copy(q, d):
        return remote(stat_send.at[q], stat_recv.at[q, d - 1], sst_sem.at[q, d - 1],
                      rst_sem.at[q, d - 1], "wid", lax.rem(w + d, 4))

    def gather_copy(half, d):
        return remote(acts.at[half, h], acts.at[half, h], sag_sem.at[half, d - 1],
                      rag_sem.at[half, d - 1], "hid", lax.rem(h + d, 4))

    def place(owner):
        return lax.rem(owner, 2) * 2 + lax.div(owner, 2)

    def scatter_copy(half, d):
        owner = lax.rem(h + d, 4)
        return remote(rs_send.at[half, place(owner)], rs_recv.at[half, d - 1],
                      srs_sem.at[half, d - 1], rrs_sem.at[half, d - 1], "hid", owner)

    def send_stats(q, wide):
        sums = jnp.sum(wide * wide, axis=1, keepdims=True)
        stat_send[q] = jnp.broadcast_to(sums, (half_rows, 128))
        for d in (1, 2, 3):
            stat_copy(q, d).start()

    def norm_rows(q, half):
        for d in (1, 2, 3):
            stat_copy(q, d).wait()
        sums = (stat_send[q] + stat_recv[q, 0]) + (stat_recv[q, 1] + stat_recv[q, 2])
        factor = lax.rsqrt(sums[:, :1] / D + EPS)
        wide = rows[half].astype(jnp.float32)
        acts[half, h] = (wide * factor * gain_ref[...]).astype(jnp.bfloat16)
        for d in (1, 2, 3):
            gather_copy(half, d).start()

    for copy in weight_copies(0):
        copy.start()
    for half in (0, 1):
        rows[half] = x_ref[half * half_rows:(half + 1) * half_rows]
    pl.semaphore_wait(barrier, 6)
    for half in (0, 1):
        send_stats(half, rows[half].astype(jnp.float32))
    for half in (0, 1):
        norm_rows(half, half)

    def stage_copies(cc):
        ring, both = lax.rem(cc, RING), lax.rem(cc, 2 * chunks)
        half, c = lax.div(both, chunks), lax.rem(both, chunks)
        a = remote(part.at[ring, 1 - core], recv_a.at[half, c], sa_sem.at[ring],
                   ra_sem.at[both], "wid", other_core)
        b = remote(send_b.at[ring], recv_b.at[half, c], sb_sem.at[ring],
                   rb_sem.at[both], "wid", other_chip)
        hid = remote(hidden.at[half, c, core, chip], hidden.at[half, c, core, chip],
                     sh_sem.at[ring], rh_sem.at[both], "wid", other_chip)
        pair = remote(hidden.at[half, c, core], hidden.at[half, c, core],
                      sg_sem.at[ring], rg_sem.at[both], "wid", other_core)
        return ring, half, c, a, b, hid, pair

    def body(g, carry):
        @pl.when(g < total)
        def _():
            ring, half, c, a, *_ = stage_copies(g)

            @pl.when(g + 1 < total)
            def _():
                for copy in weight_copies(g + 1):
                    copy.start()

            @pl.when(g < chunks)
            def _():
                down_copy(c).start()

            @pl.when(c == 0)
            def _():
                for d in (1, 2, 3):
                    gather_copy(half, d).wait()

            slot = lax.rem(g, 2)
            for copy in weight_copies(g):
                copy.wait()
            left = acts[half].reshape(4 * half_rows, width)
            for gu in (0, 1):
                product = jnp.dot(left, wgu[slot, gu], preferred_element_type=jnp.float32)
                product = product.astype(jnp.bfloat16)
                for b in range(4):
                    part[ring, b % 2, b // 2, gu] = product[b * half_rows:(b + 1) * half_rows]
            a.start()

        @pl.when((g >= LAG2) & (g < total + LAG2))
        def _():
            ring, half, c, a, b, *_ = stage_copies(g - LAG2)
            a.wait()
            send_b[ring] = (
                part[ring, core, 1 - chip].astype(jnp.float32)
                + recv_a[half, c, 1 - chip].astype(jnp.float32)
            ).astype(jnp.bfloat16)
            b.start()

        @pl.when((g >= LAG3) & (g < total + LAG3))
        def _():
            ring, half, c, a, b, hid, _ = stage_copies(g - LAG3)
            b.wait()
            sums = (
                part[ring, core, chip].astype(jnp.float32)
                + recv_a[half, c, chip].astype(jnp.float32)
            ) + recv_b[half, c].astype(jnp.float32)
            gate, up = sums[0], sums[1]
            hidden[half, c, core, chip] = (gate / (1.0 + jnp.exp(-gate)) * up).astype(jnp.bfloat16)
            hid.start()

        @pl.when((g >= LAG4) & (g < total + LAG4))
        def _():
            *_, hid, pair = stage_copies(g - LAG4)
            hid.wait()
            pair.start()

        @pl.when((g >= LAG5) & (g < total + LAG5))
        def _():
            cc = g - LAG5
            ring, half, c, *_, pair = stage_copies(cc)

            @pl.when(cc < chunks)
            def _():
                down_copy(c).wait()

            @pl.when(c == 0)
            def _():
                acc[...] = jnp.zeros_like(acc)

            pair.wait()
            left = hidden[half, c].reshape(4 * half_rows, UNITS)
            for n in range(0, width, 512):
                acc[:, n:n + 512] += jnp.dot(
                    left, wd[c, :, n:n + 512], preferred_element_type=jnp.float32
                )

            @pl.when(c == chunks - 1)
            def _():
                rs_send[half] = acc[...].astype(jnp.bfloat16).reshape(4, half_rows, width)
                for d in (1, 2, 3):
                    scatter_copy(half, d).start()

        for q in range(4):
            half = q % 2
            at = q * chunks + chunks - 1 + LAG5 + LAG_ROWS

            @pl.when(g == at)
            def _():
                for d in (1, 2, 3):
                    scatter_copy(half, d).wait()
                branch = rs_send[half, place(h)].astype(jnp.float32)
                for d in (1, 2, 3):
                    branch = branch + rs_recv[half, d - 1].astype(jnp.float32)
                new = (rows[half].astype(jnp.float32) + branch).astype(jnp.bfloat16)
                if q < 2:
                    rows[half] = new
                    send_stats(q + 2, new.astype(jnp.float32))
                else:
                    out_ref[half * half_rows:(half + 1) * half_rows] = new

            if q < 2:
                @pl.when(g == at + LAG_NORM)
                def _():
                    norm_rows(q + 2, half)

        return carry

    lax.fori_loop(0, total + LAG5 + LAG_ROWS, body, 0)


def kernel_body(activations, norm_gain, gate_weight, up_weight, down_weight):
    own_rows, width = activations.shape
    chunks = gate_weight.shape[1] // UNITS
    hr = own_rows // 2
    bf, f32, dma = jnp.bfloat16, jnp.float32, pltpu.SemaphoreType.DMA
    vmem, hbm = pl.BlockSpec(memory_space=pltpu.VMEM), pl.BlockSpec(memory_space=pl.ANY)
    flops = 2 * 2 * 3 * 4 * own_rows * width * gate_weight.shape[1]
    return pl.pallas_call(
        functools.partial(kernel, chunks),
        out_shape=jax.ShapeDtypeStruct((own_rows, width), bf),
        in_specs=[vmem, vmem, hbm, hbm, hbm],
        out_specs=vmem,
        scratch_shapes=[
            pltpu.VMEM((2, 2, width, UNITS), bf),
            pltpu.VMEM((chunks, UNITS, width), bf),
            pltpu.VMEM((2, hr, width), bf),
            pltpu.VMEM((2, 4, hr, width), bf),
            pltpu.VMEM((RING, 2, 2, 2, hr, UNITS), bf),
            pltpu.VMEM((2, chunks, 2, 2, hr, UNITS), bf),
            pltpu.VMEM((RING, 2, hr, UNITS), bf),
            pltpu.VMEM((2, chunks, 2, hr, UNITS), bf),
            pltpu.VMEM((2, chunks, 2, 2, hr, UNITS), bf),
            pltpu.VMEM((4 * hr, width), f32),
            pltpu.VMEM((2, 4, hr, width), bf),
            pltpu.VMEM((2, 3, hr, width), bf),
            pltpu.VMEM((4, hr, 128), f32),
            pltpu.VMEM((4, 3, hr, 128), f32),
            dma((2, 2)), dma((chunks,)),
            dma((RING,)), dma((2 * chunks,)), dma((RING,)), dma((2 * chunks,)),
            dma((RING,)), dma((2 * chunks,)), dma((RING,)), dma((2 * chunks,)),
            dma((2, 3)), dma((2, 3)), dma((2, 3)), dma((2, 3)), dma((4, 3)), dma((4, 3)),
        ],
        compiler_params=pltpu.CompilerParams(
            collective_id=0, has_side_effects=True, vmem_limit_bytes=62 * 1024 * 1024
        ),
        cost_estimate=pl.CostEstimate(
            flops=flops, bytes_accessed=10 * gate_weight.size, transcendentals=0
        ),
    )(activations, norm_gain[None, :], gate_weight, up_weight, down_weight)


def solution(mesh):
    placed = (
        P(("groups", "hid"), "wid"),
        P("wid"),
        P("wid", "hid"),
        P("wid", "hid"),
        P("hid", "wid"),
    )

    def body(activations, norm_gain, gate_weight, up_weight, down_weight):
        fits = (
            mesh.shape["wid"] == 4 and mesh.shape["hid"] == 4
            and activations.shape == (64, 2048) and gate_weight.shape[1] == 14 * UNITS
        )
        form = kernel_body if fits else plain_body
        return form(activations, norm_gain, gate_weight, up_weight, down_weight)

    return jax.shard_map(
        body, mesh=mesh, in_specs=placed, out_specs=P(("groups", "hid"), "wid"), check_vma=False
    )
```

```python
import functools

import jax
import jax.numpy as jnp
from jax import lax
from jax.experimental import pallas as pl
from jax.experimental.pallas import tpu as pltpu
from jax.sharding import PartitionSpec as P

D = 8192
EPS = 1e-05
UNITS = 512
LAG2, LAG3, LAG4, LAG5 = 1, 3, 5, 6
LAG_ROWS, LAG_NORM = 4, 2
GAP = 3
RING = 8


def normed(values, norm_gain):
    wide = values.astype(jnp.float32)
    partial_sq = jnp.sum(wide * wide, axis=1)
    total_sq = lax.psum(partial_sq, "wid")
    factor = lax.rsqrt(total_sq / D + EPS)
    return (wide * factor[:, None] * norm_gain[None, :]).astype(jnp.bfloat16)


def project_local(inputs, gate_weight, up_weight):
    gate_part = jnp.dot(inputs, gate_weight, preferred_element_type=jnp.float32)
    up_part = jnp.dot(inputs, up_weight, preferred_element_type=jnp.float32)
    return jnp.stack([gate_part, up_part]).astype(jnp.bfloat16).astype(jnp.float32)


def combine_hidden(partials):
    shared = lax.psum_scatter(
        partials.astype(jnp.bfloat16), "wid", scatter_dimension=2, tiled=True
    ).astype(jnp.float32)
    hidden_share = (jax.nn.silu(shared[0]) * shared[1]).astype(jnp.bfloat16)
    return lax.all_gather(hidden_share, "wid", axis=1, tiled=True)


def hidden_from_share(normed_share, gate_weight, up_weight):
    partials = project_local(
        lax.all_gather(normed_share, "hid", axis=0, tiled=True), gate_weight, up_weight
    )
    return combine_hidden(partials)


def down_share(hidden, down_weight):
    return lax.psum_scatter(
        jnp.dot(hidden, down_weight, preferred_element_type=jnp.float32).astype(jnp.bfloat16),
        "hid",
        scatter_dimension=0,
        tiled=True,
    ).astype(jnp.float32)


def plain_body(activations, norm_gain, gate_weight, up_weight, down_weight):
    first_hidden = hidden_from_share(normed(activations, norm_gain), gate_weight, up_weight)
    first_own = (activations.astype(jnp.float32) + down_share(first_hidden, down_weight)).astype(
        jnp.bfloat16
    )
    second_hidden = hidden_from_share(normed(first_own, norm_gain), gate_weight, up_weight)
    second_branch = down_share(second_hidden, down_weight)
    return (first_own.astype(jnp.float32) + second_branch).astype(jnp.bfloat16)


def kernel(
    chunks, x_ref, gain_ref, wg_hbm, wu_hbm, wd_hbm, out_ref,
    wgu, wd, rows, acts, part, recv_a, send_b, recv_b, hidden, acc, rs_send, rs_recv,
    stat_send, stat_recv,
    w_sem, wd_sem, sa_sem, ra_sem, sb_sem, rb_sem, sh_sem, rh_sem, sg_sem, rg_sem,
    srs_sem, rrs_sem, sag_sem, rag_sem, sst_sem, rst_sem,
):
    total = 4 * chunks
    h = lax.axis_index("hid")
    w = lax.axis_index("wid")
    chip, core = lax.div(w, 2), lax.rem(w, 2)
    other_core = 2 * chip + (1 - core)
    other_chip = 2 * (1 - chip) + core
    half_rows = rows.shape[1]
    width = rows.shape[2]

    def remote(src, dst, send, recv, axis, peer):
        return pltpu.make_async_remote_copy(
            src_ref=src, dst_ref=dst, send_sem=send, recv_sem=recv,
            device_id={axis: peer}, device_id_type=pl.DeviceIdType.MESH,
        )

    barrier = pltpu.get_barrier_semaphore()
    for d in (1, 2, 3):
        pl.semaphore_signal(barrier, inc=1, device_id={"wid": lax.rem(w + d, 4)},
                            device_id_type=pl.DeviceIdType.MESH)
        pl.semaphore_signal(barrier, inc=1, device_id={"hid": lax.rem(h + d, 4)},
                            device_id_type=pl.DeviceIdType.MESH)

    def weight_copies(g):
        columns = pl.ds(pl.multiple_of(lax.rem(g, chunks) * UNITS, UNITS), UNITS)
        slot = lax.rem(g, 2)
        return (
            pltpu.make_async_copy(wg_hbm.at[:, columns], wgu.at[slot, 0], w_sem.at[slot, 0]),
            pltpu.make_async_copy(wu_hbm.at[:, columns], wgu.at[slot, 1], w_sem.at[slot, 1]),
        )

    def down_copy(c):
        span = pl.ds(pl.multiple_of(c * UNITS, UNITS), UNITS)
        return pltpu.make_async_copy(wd_hbm.at[span, :], wd.at[c], wd_sem.at[c])

    def stat_copy(q, d):
        return remote(stat_send.at[q], stat_recv.at[q, d - 1], sst_sem.at[q, d - 1],
                      rst_sem.at[q, d - 1], "wid", lax.rem(w + d, 4))

    def gather_copy(half, d):
        return remote(acts.at[half, h], acts.at[half, h], sag_sem.at[half, d - 1],
                      rag_sem.at[half, d - 1], "hid", lax.rem(h + d, 4))

    def place(owner):
        return lax.rem(owner, 2) * 2 + lax.div(owner, 2)

    def scatter_copy(half, d):
        owner = lax.rem(h + d, 4)
        return remote(rs_send.at[half, place(owner)], rs_recv.at[half, d - 1],
                      srs_sem.at[half, d - 1], rrs_sem.at[half, d - 1], "hid", owner)

    def send_stats(q, wide):
        sums = jnp.sum(wide * wide, axis=1, keepdims=True)
        stat_send[q] = jnp.broadcast_to(sums, (half_rows, 128))
        for d in (1, 2, 3):
            stat_copy(q, d).start()

    def norm_rows(q, half):
        for d in (1, 2, 3):
            stat_copy(q, d).wait()
        sums = (stat_send[q] + stat_recv[q, 0]) + (stat_recv[q, 1] + stat_recv[q, 2])
        factor = lax.rsqrt(sums[:, :1] / D + EPS)
        wide = rows[half].astype(jnp.float32)
        acts[half, h] = (wide * factor * gain_ref[...]).astype(jnp.bfloat16)
        for d in (1, 2, 3):
            gather_copy(half, d).start()

    for copy in weight_copies(0):
        copy.start()
    for half in (0, 1):
        rows[half] = x_ref[half * half_rows:(half + 1) * half_rows]
    pl.semaphore_wait(barrier, 6)
    for half in (0, 1):
        send_stats(half, rows[half].astype(jnp.float32))
    norm_rows(0, 0)

    def chunk_at(time):
        step, inner = lax.div(time, 2 * chunks + GAP), lax.rem(time, 2 * chunks + GAP)
        cc = step * (2 * chunks) + inner
        return cc, (time >= 0) & (inner < 2 * chunks) & (cc < total)

    def stage_copies(cc):
        ring, both = lax.rem(cc, RING), lax.rem(cc, 2 * chunks)
        half, c = lax.div(both, chunks), lax.rem(both, chunks)
        a = remote(part.at[ring, 1 - core], recv_a.at[half, c], sa_sem.at[ring],
                   ra_sem.at[both], "wid", other_core)
        b = remote(send_b.at[ring], recv_b.at[half, c], sb_sem.at[ring],
                   rb_sem.at[both], "wid", other_chip)
        hid = remote(hidden.at[half, c, core, chip], hidden.at[half, c, core, chip],
                     sh_sem.at[ring], rh_sem.at[both], "wid", other_chip)
        pair = remote(hidden.at[half, c, core], hidden.at[half, c, core],
                      sg_sem.at[ring], rg_sem.at[both], "wid", other_core)
        return ring, half, c, a, b, hid, pair

    def body(g, carry):
        cc1, active1 = chunk_at(g)
        cc2, active2 = chunk_at(g - LAG2)
        cc3, active3 = chunk_at(g - LAG3)
        cc4, active4 = chunk_at(g - LAG4)
        cc5, active5 = chunk_at(g - LAG5)

        @pl.when(active1)
        def _():
            ring, half, c, a, *_ = stage_copies(cc1)

            @pl.when(cc1 + 1 < total)
            def _():
                for copy in weight_copies(cc1 + 1):
                    copy.start()

            @pl.when(cc1 < chunks)
            def _():
                down_copy(c).start()

            @pl.when(c == 0)
            def _():
                for d in (1, 2, 3):
                    gather_copy(half, d).wait()

            @pl.when(cc1 == 0)
            def _():
                norm_rows(1, 1)

            slot = lax.rem(cc1, 2)
            for copy in weight_copies(cc1):
                copy.wait()
            left = acts[half].reshape(4 * half_rows, width)
            for gu in (0, 1):
                product = jnp.dot(left, wgu[slot, gu], preferred_element_type=jnp.float32)
                product = product.astype(jnp.bfloat16)
                for b in range(4):
                    part[ring, b % 2, b // 2, gu] = product[b * half_rows:(b + 1) * half_rows]
            a.start()

        @pl.when(active2)
        def _():
            ring, half, c, a, b, *_ = stage_copies(cc2)
            a.wait()
            send_b[ring] = (
                part[ring, core, 1 - chip].astype(jnp.float32)
                + recv_a[half, c, 1 - chip].astype(jnp.float32)
            ).astype(jnp.bfloat16)
            b.start()

        @pl.when(active3)
        def _():
            ring, half, c, a, b, hid, _ = stage_copies(cc3)
            b.wait()
            sums = (
                part[ring, core, chip].astype(jnp.float32)
                + recv_a[half, c, chip].astype(jnp.float32)
            ) + recv_b[half, c].astype(jnp.float32)
            gate, up = sums[0], sums[1]
            hidden[half, c, core, chip] = (gate / (1.0 + jnp.exp(-gate)) * up).astype(jnp.bfloat16)
            hid.start()

        @pl.when(active4)
        def _():
            *_, hid, pair = stage_copies(cc4)
            hid.wait()
            pair.start()

        @pl.when(active5)
        def _():
            ring, half, c, *_, pair = stage_copies(cc5)

            @pl.when(cc5 < chunks)
            def _():
                down_copy(c).wait()

            @pl.when(c == 0)
            def _():
                acc[...] = jnp.zeros_like(acc)

            pair.wait()
            left = hidden[half, c].reshape(4 * half_rows, UNITS)
            for n in range(0, width, 512):
                acc[:, n:n + 512] += jnp.dot(
                    left, wd[c, :, n:n + 512], preferred_element_type=jnp.float32
                )

            @pl.when(c == chunks - 1)
            def _():
                rs_send[half] = acc[...].astype(jnp.bfloat16).reshape(4, half_rows, width)
                for d in (1, 2, 3):
                    scatter_copy(half, d).start()

        for q in range(4):
            half = q % 2
            at = q * chunks + (q // 2) * GAP + chunks - 1 + LAG5 + LAG_ROWS

            @pl.when(g == at)
            def _():
                for d in (1, 2, 3):
                    scatter_copy(half, d).wait()
                branch = rs_send[half, place(h)].astype(jnp.float32)
                for d in (1, 2, 3):
                    branch = branch + rs_recv[half, d - 1].astype(jnp.float32)
                new = (rows[half].astype(jnp.float32) + branch).astype(jnp.bfloat16)
                if q < 2:
                    rows[half] = new
                    send_stats(q + 2, new.astype(jnp.float32))
                else:
                    out_ref[half * half_rows:(half + 1) * half_rows] = new

            if q < 2:
                @pl.when(g == at + LAG_NORM)
                def _():
                    norm_rows(q + 2, half)

        return carry

    lax.fori_loop(0, total + GAP + LAG5 + LAG_ROWS, body, 0)


def kernel_body(activations, norm_gain, gate_weight, up_weight, down_weight):
    own_rows, width = activations.shape
    chunks = gate_weight.shape[1] // UNITS
    hr = own_rows // 2
    bf, f32, dma = jnp.bfloat16, jnp.float32, pltpu.SemaphoreType.DMA
    vmem, hbm = pl.BlockSpec(memory_space=pltpu.VMEM), pl.BlockSpec(memory_space=pl.ANY)
    flops = 2 * 2 * 3 * 4 * own_rows * width * gate_weight.shape[1]
    return pl.pallas_call(
        functools.partial(kernel, chunks),
        out_shape=jax.ShapeDtypeStruct((own_rows, width), bf),
        in_specs=[vmem, vmem, hbm, hbm, hbm],
        out_specs=vmem,
        scratch_shapes=[
            pltpu.VMEM((2, 2, width, UNITS), bf),
            pltpu.VMEM((chunks, UNITS, width), bf),
            pltpu.VMEM((2, hr, width), bf),
            pltpu.VMEM((2, 4, hr, width), bf),
            pltpu.VMEM((RING, 2, 2, 2, hr, UNITS), bf),
            pltpu.VMEM((2, chunks, 2, 2, hr, UNITS), bf),
            pltpu.VMEM((RING, 2, hr, UNITS), bf),
            pltpu.VMEM((2, chunks, 2, hr, UNITS), bf),
            pltpu.VMEM((2, chunks, 2, 2, hr, UNITS), bf),
            pltpu.VMEM((4 * hr, width), f32),
            pltpu.VMEM((2, 4, hr, width), bf),
            pltpu.VMEM((2, 3, hr, width), bf),
            pltpu.VMEM((4, hr, 128), f32),
            pltpu.VMEM((4, 3, hr, 128), f32),
            dma((2, 2)), dma((chunks,)),
            dma((RING,)), dma((2 * chunks,)), dma((RING,)), dma((2 * chunks,)),
            dma((RING,)), dma((2 * chunks,)), dma((RING,)), dma((2 * chunks,)),
            dma((2, 3)), dma((2, 3)), dma((2, 3)), dma((2, 3)), dma((4, 3)), dma((4, 3)),
        ],
        compiler_params=pltpu.CompilerParams(
            collective_id=0, has_side_effects=True, vmem_limit_bytes=62 * 1024 * 1024
        ),
        cost_estimate=pl.CostEstimate(
            flops=flops, bytes_accessed=10 * gate_weight.size, transcendentals=0
        ),
    )(activations, norm_gain[None, :], gate_weight, up_weight, down_weight)


def solution(mesh):
    placed = (
        P(("groups", "hid"), "wid"),
        P("wid"),
        P("wid", "hid"),
        P("wid", "hid"),
        P("hid", "wid"),
    )

    def body(activations, norm_gain, gate_weight, up_weight, down_weight):
        fits = (
            mesh.shape["wid"] == 4 and mesh.shape["hid"] == 4
            and activations.shape == (64, 2048) and gate_weight.shape[1] == 14 * UNITS
        )
        form = kernel_body if fits else plain_body
        return form(activations, norm_gain, gate_weight, up_weight, down_weight)

    return jax.shard_map(
        body, mesh=mesh, in_specs=placed, out_specs=P(("groups", "hid"), "wid"), check_vma=False
    )
```
